32 devices in a mesh: row: 4 (over y, x), col: 8 (over z, core).
Axes of the slice: x: 2, y: 2, z: 4, core: 2. Of those that a mesh axis runs over, the one named last changes fastest.
Arguments:
- amplitudes: float32 [4096, 3072], P('row', 'col'), may hold values from -6 to 6
- integrals: float32 [3072, 3072], P('row', 'col'), may hold values from -0.3125 to 0.3125
- pair_irrep: int32 [3072], replicated, may hold values from 0 to 7, as said below
- occ_gap: float32 [4096], P('row'), may hold values from 0.5 to 4
- virt_gap: float32 [3072], P('col'), may hold values from 0.5 to 4
Outputs:
- update: float32 [4096, 3072], P('row', 'col')
The draws below stay inside these ranges and needn't reach their ends.
Inputs may be any that keep to these rules, and one draw needn't show every extreme that they name: `pair_irrep`: split the virtual pairs into aligned blocks, one per index of the row axis, each of 3072 // (number of row indices) pairs; every irrep occurs equally often in each block.
All inputs are finite; a program needn't handle non-finite values.
Results may differ from the reference program's by a relative error of at most 0.000078.
Values sent between devices are 32-bit elements; how exact they have to be, the bound alone decides.
A program may use at most 128 MiB of HBM per device.

```python
import math
import jax
import jax.numpy as jnp
from jax import lax

IRREPS = 8
OCC_PAIRS = 4096
PAIRS = 3072
N_ROW = 4


def draw_pair_irrep(key, part):
    key = jax.random.fold_in(key, 11)
    block_len = PAIRS // N_ROW
    labels = jnp.arange(block_len, dtype=jnp.int32) % IRREPS
    block_keys = jax.random.split(key, N_ROW)
    shuffled = jax.vmap(lambda k: jax.random.permutation(k, labels))(block_keys)
    return shuffled.reshape(PAIRS).astype(jnp.int32)


def block_levels(key, extent, pieces, least, largest):
    factor_of = 1.0
    for position, blocks in pieces:
        heights = jax.random.uniform(jax.random.fold_in(jax.random.fold_in(key, 6), position), (blocks,), jnp.float32, least / len(pieces), largest / len(pieces))
        factor_of = factor_of * jnp.repeat(jnp.exp(heights), extent[position] // blocks).reshape((-1,) + (1,) * (len(extent) - 1 - position))
    return factor_of


def centred(key, dims, width, limit, shards=(), held_as=jnp.bfloat16):
    drawn = width * jax.random.normal(key, dims, jnp.float32)
    if shards:
        drawn = drawn * block_levels(key, dims, shards, -0.22, 0.18)
    return jnp.clip(drawn, -limit, limit).astype(held_as)


def setup_inputs(seed: int = 0) -> dict:
    seeds = jax.random.split(jax.random.key(seed), 6)
    return {
        "amplitudes": centred(seeds[0], (OCC_PAIRS, PAIRS), 1.0, 6.0, ((0, 4), (1, 8)), jnp.float32),
        "integrals": centred(seeds[1], (PAIRS, PAIRS), (PAIRS // 8) ** -0.5, 0.3125, ((0, 4), (1, 8)), jnp.float32),
        "pair_irrep": draw_pair_irrep(jax.random.fold_in(seeds[5], 71), 0),
        "occ_gap": jnp.clip(jnp.exp(math.log(4.0) - 2.0794415 * jax.random.uniform(seeds[3], (OCC_PAIRS,), jnp.float32) ** block_levels(seeds[3], (OCC_PAIRS,), ((0, 4),), -0.2, 0.2)), 0.5, 4.0),
        "virt_gap": jnp.clip(jnp.exp(math.log(4.0) - 2.0794415 * jax.random.uniform(seeds[4], (PAIRS,), jnp.float32) ** block_levels(seeds[4], (PAIRS,), ((0, 8),), -0.2, 0.2)), 0.5, 4.0),
    }


def reference(amplitudes, integrals, pair_irrep, occ_gap, virt_gap):
    same = pair_irrep[:, None] == pair_irrep[None, :]
    blocked = jnp.where(same, integrals, jnp.float32(0.0))
    ladder = jnp.dot(amplitudes, blocked, preferred_element_type=jnp.float32, precision=lax.Precision.HIGHEST)
    return ladder / (occ_gap[:, None] + virt_gap[None, :])
```

```python
import functools

import jax
import jax.numpy as jnp
from jax import lax
from jax.experimental import pallas as pl
from jax.experimental.pallas import tpu as pltpu
from jax.sharding import PartitionSpec as P

IRREPS = 8
MESH = pl.DeviceIdType.MESH
BF16, F32 = jnp.bfloat16, jnp.float32
NN = (((1,), (0,)), ((), ()))
NT = (((1,), (1,)), ((), ()))


def split(x):
    high = x.astype(BF16)
    return high, (x - high.astype(F32)).astype(BF16)


def dot(a, b, dims=NN):
    return lax.dot_general(a, b, dims, preferred_element_type=F32)


def kernel(sizes, a_ref, v_ref, irr_ref, out_ref, pos, pick, own, own_t, apart, fsend, frecv, lsend, lpart,
           vsrc, vin, vsum, vg, vhigh, vlow, *sems):
    R, q, G, T, b, bp, nch, rc, n_loc, nb = sizes
    a_s, a_r, f_s, f_r, l_s, l_r, o_s, o_r, x_s, x_r, z_s, z_r, r_s, r_r = sems
    r, c = lax.axis_index("row"), lax.axis_index("col")
    z, s = c // q, c % q
    half = R * b

    def in_group(d):
        return (r, z * q + (s + d) % q)

    def in_line(d):
        return (r, ((z + d) % R) * q + s)

    def in_plane(d):
        return ((r + d) % R, c)

    def remote(src, dst, send, recv, target):
        return pltpu.make_async_remote_copy(
            src_ref=src, dst_ref=dst, send_sem=send, recv_sem=recv, device_id=target, device_id_type=MESH)

    def a_copy(i, d):
        return remote(a_ref.at[((s + d) % q) // G, i], apart.at[s, i], a_s.at[i, d], a_r.at[i, d], in_group(d))

    def f_copy(i, d):
        return remote(fsend.at[i, (z + d) % R], frecv.at[i, z], f_s.at[i, d], f_r.at[i, d], in_line(d))

    def l_copy(i, d):
        return remote(lsend.at[i, (z + d) % R], lpart.at[s, i, z], l_s.at[i, d], l_r.at[i, d], in_line(d))

    def o_copy(i, d):
        return remote(lpart.at[s, i], lpart.at[s, i], o_s.at[i, d], o_r.at[i, d], in_group(d))

    def x_copy(d):
        return remote(vsrc.at[((s + d) % q) % G], vin.at[s], x_s.at[d], x_r.at[d], in_group(d))

    def z_copy(d):
        return remote(vsum.at[(z + d) % R], vg.at[r, z], z_s.at[d], z_r.at[d], in_line(d))

    def r_copy(d):
        return remote(vg.at[r], vg.at[r], r_s.at[d], r_r.at[d], in_plane(d))

    barrier = pltpu.get_barrier_semaphore()
    for d in range(1, q):
        pl.semaphore_signal(barrier, inc=1, device_id=in_group(d), device_id_type=MESH)
    for d in range(1, R):
        pl.semaphore_signal(barrier, inc=1, device_id=in_line(d), device_id_type=MESH)
        pl.semaphore_signal(barrier, inc=1, device_id=in_plane(d), device_id_type=MESH)
    pl.semaphore_wait(barrier, q - 1 + 2 * (R - 1))

    @pl.loop(0, nch)
    def _(i):
        for d in range(1, q):
            a_copy(i, d).start()
        apart[s, i] = a_ref[s // G, i]

    before = (lax.broadcasted_iota(jnp.int32, (nb, nb), 0) < lax.broadcasted_iota(jnp.int32, (nb, nb), 1)).astype(F32).astype(BF16)

    def slots(block):
        labels = irr_ref[pl.ds(block, 1), :]
        mine = (lax.broadcasted_iota(jnp.int32, (IRREPS, nb), 0) == labels).astype(F32)
        rank = jnp.sum(mine * dot(mine.astype(BF16), before), axis=0, keepdims=True).astype(jnp.int32)
        return (labels % G) * half + (labels // G) * b + rank

    pos_n = slots(z)
    pos[0:1, :] = pos_n
    pick[...] = (lax.broadcasted_iota(jnp.int32, (half, nb), 0) + (s % G) * half == pos_n).astype(F32).astype(BF16)

    def forward(i):
        for d in range(1, q):
            a_copy(i, d).wait_recv()
        total = jnp.zeros((half, rc), F32)
        for j in range(q):
            high, low = split(apart[j, i])
            chosen = pick[:, j * n_loc:(j + 1) * n_loc]
            total += dot(chosen, high, NT) + dot(chosen, low, NT)
        fsend[i] = total.reshape(R, b, rc)
        for d in range(1, R):
            f_copy(i, d).start()
        frecv[i, z] = fsend[i, z]

    forward(0)

    pos_own = pos[0:1, pl.ds(pl.multiple_of(s * n_loc, 128), n_loc)]
    own_f = (lax.broadcasted_iota(jnp.int32, (IRREPS * b, n_loc), 0) == pos_own).astype(F32)
    own[...] = own_f.astype(BF16)
    pos_k = slots(r)
    v_high, v_low = split(v_ref[...])
    vsrc[...] = jnp.zeros_like(vsrc)
    for p in range(G):
        rows = (lax.broadcasted_iota(jnp.int32, (half, nb), 0) + p * half == pos_k).astype(F32).astype(BF16)
        sorted_v = dot(rows, v_high) + dot(rows, v_low)
        for j in range(R):
            high, low = split(sorted_v[j * b:(j + 1) * b, :])
            chosen = own[p * half + j * b:p * half + (j + 1) * b, :]
            vsrc[p, j, :, 0:b] = dot(chosen, high, NT) + dot(chosen, low, NT)
    for d in range(1, q):
        x_copy(d).start()
    vin[s] = vsrc[s % G]

    @pl.loop(1, nch // 2)
    def _(i):
        forward(i)

    for d in range(1, q):
        x_copy(d).wait_recv()
    block = vin[0]
    for j in range(1, q):
        block += vin[j]
    vsum[...] = block
    for d in range(1, R):
        z_copy(d).start()
    vg[r, z] = vsum[z]

    @pl.loop(nch // 2, nch)
    def _(i):
        forward(i)

    own_t[...] = own_f.T.astype(BF16)
    for d in range(1, R):
        z_copy(d).wait_recv()
    for d in range(1, R):
        r_copy(d).start()
    for d in range(1, R):
        r_copy(d).wait_recv()
    whole = jnp.concatenate([vg[j].reshape(half, bp)[:, :b] for j in range(R)], axis=1)
    high, low = split(whole)
    vhigh[...] = high
    vlow[...] = low

    @pl.loop(0, nch)
    def _(i):
        for d in range(1, R):
            f_copy(i, d).wait_recv()
        high, low = split(frecv[i].reshape(half, rc))
        total = dot(vhigh[...], high) + (dot(vhigh[...], low) + dot(vlow[...], high))
        lsend[i] = total.reshape(R, b, rc)
        for d in range(1, R):
            l_copy(i, d).start()
        lpart[s, i, z] = lsend[i, z]

    def share(i):
        for d in range(1, R):
            l_copy(i, d).wait_recv()
        for d in range(1, q):
            o_copy(i, d).start()

    def finish(i):
        for d in range(1, q):
            o_copy(i, d).wait_recv()
        for t in range(T):
            total = jnp.zeros((n_loc, rc), F32)
            for p in range(G):
                high, low = split(lpart[t * G + p, i].reshape(half, rc))
                chosen = own_t[:, p * half:(p + 1) * half]
                total += dot(chosen, high) + dot(chosen, low)
            out_ref[t, i] = total.T

    share(0)

    @pl.loop(1, nch)
    def _(i):
        share(i)
        finish(i - 1)

    finish(nch - 1)

    @pl.loop(0, nch)
    def _(i):
        for d in range(1, q):
            a_copy(i, d).wait_send()
            o_copy(i, d).wait_send()
        for d in range(1, R):
            f_copy(i, d).wait_send()
            l_copy(i, d).wait_send()

    for d in range(1, q):
        x_copy(d).wait_send()
    for d in range(1, R):
        z_copy(d).wait_send()
        r_copy(d).wait_send()


def body(R, C, amplitudes, integrals, pair_irrep, occ_gap, virt_gap):
    rows, n_loc = amplitudes.shape
    nb = integrals.shape[0]
    q, G = C // R, IRREPS // R
    T = q // G
    b = nb // IRREPS
    bp = -(-b // 128) * 128
    rc = 256
    nch = rows // T // rc
    half = R * b
    sizes = (R, q, G, T, b, bp, nch, rc, n_loc, nb)
    dma = pltpu.SemaphoreType.DMA
    ladder = pl.pallas_call(
        functools.partial(kernel, sizes),
        out_shape=jax.ShapeDtypeStruct((T, nch, rc, n_loc), F32),
        in_specs=[pl.BlockSpec(memory_space=pltpu.VMEM)] * 3,
        out_specs=pl.BlockSpec(memory_space=pltpu.VMEM),
        scratch_shapes=[
            pltpu.VMEM((8, nb), jnp.int32),
            pltpu.VMEM((half, nb), BF16),
            pltpu.VMEM((IRREPS * b, n_loc), BF16),
            pltpu.VMEM((n_loc, IRREPS * b), BF16),
            pltpu.VMEM((q, nch, rc, n_loc), F32),
            pltpu.VMEM((nch, R, b, rc), F32),
            pltpu.VMEM((nch, R, b, rc), F32),
            pltpu.VMEM((nch, R, b, rc), F32),
            pltpu.VMEM((q, nch, R, b, rc), F32),
            pltpu.VMEM((G, R, b, bp), F32),
            pltpu.VMEM((q, R, b, bp), F32),
            pltpu.VMEM((R, b, bp), F32),
            pltpu.VMEM((R, R, b, bp), F32),
            pltpu.VMEM((half, half), BF16),
            pltpu.VMEM((half, half), BF16),
        ] + [dma((nch, q))] * 2 + [dma((nch, R))] * 4 + [dma((nch, q))] * 2 + [dma((q,))] * 2 + [dma((R,))] * 4,
        compiler_params=pltpu.CompilerParams(
            collective_id=0, has_side_effects=True, vmem_limit_bytes=60 * 2**20),
    )(amplitudes.reshape(T, nch, rc, n_loc), integrals, pair_irrep.reshape(R, nb))
    return ladder.reshape(rows, n_loc) / (occ_gap[:, None] + virt_gap[None, :])


def solution(mesh):
    placed = (P("row", "col"), P("row", "col"), P(), P("row"), P("col"))
    return jax.shard_map(
        functools.partial(body, mesh.shape["row"], mesh.shape["col"]),
        mesh=mesh, in_specs=placed, out_specs=P("row", "col"), check_vma=False,
    )
```

```python
import functools

import jax
import jax.numpy as jnp
from jax import lax
from jax.experimental import pallas as pl
from jax.experimental.pallas import tpu as pltpu
from jax.sharding import PartitionSpec as P

IRREPS = 8
MESH = pl.DeviceIdType.MESH
BF16, F32 = jnp.bfloat16, jnp.float32
NN = (((1,), (0,)), ((), ()))
NT = (((1,), (1,)), ((), ()))


def split(x):
    high = x.astype(BF16)
    return high, (x - high.astype(F32)).astype(BF16)


def dot(a, b, dims=NN):
    return lax.dot_general(a, b, dims, preferred_element_type=F32)


def kernel(sizes, a_ref, v_ref, irr_ref, occ_ref, virt_ref, out_ref, pos, pick, own, own_t, apart, fsend, frecv, lsend, lpart,
           vsrc, vin, vsum, vg, vhigh, vlow, v_in, stage, *sems):
    R, q, G, T, b, bp, nch, rc, n_loc, nb = sizes
    a_s, a_r, f_s, f_r, l_s, l_r, o_s, o_r, x_s, x_r, z_s, z_r, r_s, r_r, own_sem, v_sem, out_sem = sems
    r, c = lax.axis_index("row"), lax.axis_index("col")
    z, s = c // q, c % q
    half = R * b

    def in_group(d):
        return (r, z * q + (s + d) % q)

    def across(d):
        if R & (R - 1):
            return (z + d) % R
        flips = [w for w in (2**k for k in range(R.bit_length())) if (R - d) & w]
        return z + sum(w - 2 * w * ((z // w) % 2) for w in flips)

    def in_line(d):
        return (r, across(d) * q + s)

    def in_plane(d):
        return ((r + d) % R, c)

    def remote(src, dst, send, recv, target):
        return pltpu.make_async_remote_copy(
            src_ref=src, dst_ref=dst, send_sem=send, recv_sem=recv, device_id=target, device_id_type=MESH)

    def a_copy(i, d):
        return remote(a_ref.at[((s + d) % q) // G, i], apart.at[s, i], a_s.at[i, d], a_r.at[i, d], in_group(d))

    def f_copy(i, d):
        return remote(fsend.at[i, across(d)], frecv.at[i, z], f_s.at[i, d], f_r.at[i, d], in_line(d))

    def l_copy(i, d):
        return remote(lsend.at[i, across(d)], lpart.at[s, i, z], l_s.at[i, d], l_r.at[i, d], in_line(d))

    def o_copy(i, d):
        return remote(lpart.at[s, i], lpart.at[s, i], o_s.at[i, d], o_r.at[i, d], in_group(d))

    def x_copy(d):
        return remote(vsrc.at[((s + d) % q) % G], vin.at[s], x_s.at[d], x_r.at[d], in_group(d))

    def z_copy(d):
        return remote(vsum.at[across(d)], vg.at[r, z], z_s.at[d], z_r.at[d], in_line(d))

    def r_copy(d):
        return remote(vg.at[r], vg.at[r], r_s.at[d], r_r.at[d], in_plane(d))

    def own_copy(i):
        return pltpu.make_async_copy(a_ref.at[s // G, i], apart.at[s, i], own_sem.at[i])

    def out_copy(t, i):
        return pltpu.make_async_copy(stage.at[t, i], out_ref.at[t, i], out_sem.at[t, i])

    v_copy = pltpu.make_async_copy(v_ref, v_in, v_sem)

    barrier = pltpu.get_barrier_semaphore()
    for d in range(1, q):
        pl.semaphore_signal(barrier, inc=1, device_id=in_group(d), device_id_type=MESH)
    for d in range(1, R):
        pl.semaphore_signal(barrier, inc=1, device_id=in_line(d), device_id_type=MESH)
        pl.semaphore_signal(barrier, inc=1, device_id=in_plane(d), device_id_type=MESH)
    pl.semaphore_wait(barrier, q - 1 + 2 * (R - 1))

    @pl.loop(0, nch)
    def _(i):
        for d in range(1, q):
            a_copy(i, d).start()
        own_copy(i).start()

    v_copy.start()

    before = (lax.broadcasted_iota(jnp.int32, (nb, nb), 0) < lax.broadcasted_iota(jnp.int32, (nb, nb), 1)).astype(F32).astype(BF16)

    def slots(block):
        labels = irr_ref[:, pl.ds(pl.multiple_of(block * nb, 128), nb)]
        mine = (lax.broadcasted_iota(jnp.int32, (IRREPS, nb), 0) == labels).astype(F32)
        rank = jnp.sum(mine * dot(mine.astype(BF16), before), axis=0, keepdims=True).astype(jnp.int32)
        return (labels % G) * half + (labels // G) * b + rank

    pos_n = slots(z)
    pos[0:1, :] = pos_n
    pick[...] = (lax.broadcasted_iota(jnp.int32, (half, nb), 0) + (s % G) * half == pos_n).astype(F32).astype(BF16)

    def forward(i):
        own_copy(i).wait()
        for d in range(1, q):
            a_copy(i, d).wait_recv()
        total = jnp.zeros((half, rc), F32)
        for j in range(q):
            high, low = split(apart[j, i])
            chosen = pick[:, j * n_loc:(j + 1) * n_loc]
            total += dot(chosen, high, NT) + dot(chosen, low, NT)
        fsend[i] = total.reshape(R, b, rc)
        for d in range(1, R):
            f_copy(i, d).start()
        frecv[i, z] = fsend[i, z]

    forward(0)

    pos_own = pos[0:1, pl.ds(pl.multiple_of(s * n_loc, 128), n_loc)]
    own_f = (lax.broadcasted_iota(jnp.int32, (IRREPS * b, n_loc), 0) == pos_own).astype(F32)
    own[...] = own_f.astype(BF16)
    pos_k = slots(r)
    v_copy.wait()
    v_high, v_low = split(v_in[...])
    vsrc[...] = jnp.zeros_like(vsrc)
    for p in range(G):
        rows = (lax.broadcasted_iota(jnp.int32, (half, nb), 0) + p * half == pos_k).astype(F32).astype(BF16)
        sorted_v = dot(rows, v_high) + dot(rows, v_low)
        for j in range(R):
            high, low = split(sorted_v[j * b:(j + 1) * b, :])
            chosen = own[p * half + j * b:p * half + (j + 1) * b, :]
            vsrc[p, j, :, 0:b] = dot(chosen, high, NT) + dot(chosen, low, NT)
    for d in range(1, q):
        x_copy(d).start()
    vin[s] = vsrc[s % G]

    @pl.loop(1, nch // 2)
    def _(i):
        forward(i)

    for d in range(1, q):
        x_copy(d).wait_recv()
    block = vin[0]
    for j in range(1, q):
        block += vin[j]
    vsum[...] = block
    for d in range(1, R):
        z_copy(d).start()
    vg[r, z] = vsum[z]

    @pl.loop(nch // 2, nch)
    def _(i):
        forward(i)

    own_t[...] = own_f.T.astype(BF16)
    for d in range(1, R):
        z_copy(d).wait_recv()
    for d in range(1, R):
        r_copy(d).start()
    for d in range(1, R):
        r_copy(d).wait_recv()
    whole = jnp.concatenate([vg[j].reshape(half, bp)[:, :b] for j in range(R)], axis=1)
    high, low = split(whole)
    vhigh[...] = high
    vlow[...] = low

    @pl.loop(0, nch)
    def _(i):
        for d in range(1, R):
            f_copy(i, d).wait_recv()
        high, low = split(frecv[i].reshape(half, rc))
        total = dot(vhigh[...], high) + (dot(vhigh[...], low) + dot(vlow[...], high))
        lsend[i] = total.reshape(R, b, rc)
        for d in range(1, R):
            l_copy(i, d).start()
        lpart[s, i, z] = lsend[i, z]

    virt = jnp.broadcast_to(virt_ref[...], (8, n_loc)).T[:, 0:1]

    def share(i):
        for d in range(1, R):
            l_copy(i, d).wait_recv()
        for d in range(1, q):
            o_copy(i, d).start()

    def finish(i):
        for d in range(1, q):
            o_copy(i, d).wait_recv()
        for t in range(T):
            total = jnp.zeros((n_loc, rc), F32)
            for p in range(G):
                high, low = split(lpart[t * G + p, i].reshape(half, rc))
                chosen = own_t[:, p * half:(p + 1) * half]
                total += dot(chosen, high) + dot(chosen, low)
            gap = occ_ref[:, pl.ds(pl.multiple_of((t * nch + i) * rc, 128), rc)] + virt
            stage[t, i] = (total / gap).T
            out_copy(t, i).start()

    share(0)

    @pl.loop(1, nch)
    def _(i):
        share(i)
        finish(i - 1)

    finish(nch - 1)

    @pl.loop(0, nch)
    def _(i):
        for d in range(1, q):
            a_copy(i, d).wait_send()
            o_copy(i, d).wait_send()
        for t in range(T):
            out_copy(t, i).wait()
        for d in range(1, R):
            f_copy(i, d).wait_send()
            l_copy(i, d).wait_send()

    for d in range(1, q):
        x_copy(d).wait_send()
    for d in range(1, R):
        z_copy(d).wait_send()
        r_copy(d).wait_send()


def body(R, C, amplitudes, integrals, pair_irrep, occ_gap, virt_gap):
    rows, n_loc = amplitudes.shape
    nb = integrals.shape[0]
    q, G = C // R, IRREPS // R
    T = q // G
    b = nb // IRREPS
    bp = -(-b // 128) * 128
    rc = 128
    nch = rows // T // rc
    half = R * b
    sizes = (R, q, G, T, b, bp, nch, rc, n_loc, nb)
    dma = pltpu.SemaphoreType.DMA
    update = pl.pallas_call(
        functools.partial(kernel, sizes),
        out_shape=jax.ShapeDtypeStruct((T, nch, rc, n_loc), F32),
        in_specs=[pl.BlockSpec(memory_space=pl.ANY)] * 2 + [pl.BlockSpec(memory_space=pltpu.VMEM)] * 3,
        out_specs=pl.BlockSpec(memory_space=pl.ANY),
        scratch_shapes=[
            pltpu.VMEM((8, nb), jnp.int32),
            pltpu.VMEM((half, nb), BF16),
            pltpu.VMEM((IRREPS * b, n_loc), BF16),
            pltpu.VMEM((n_loc, IRREPS * b), BF16),
            pltpu.VMEM((q, nch, rc, n_loc), F32),
            pltpu.VMEM((nch, R, b, rc), F32),
            pltpu.VMEM((nch, R, b, rc), F32),
            pltpu.VMEM((nch, R, b, rc), F32),
            pltpu.VMEM((q, nch, R, b, rc), F32),
            pltpu.VMEM((G, R, b, bp), F32),
            pltpu.VMEM((q, R, b, bp), F32),
            pltpu.VMEM((R, b, bp), F32),
            pltpu.VMEM((R, R, b, bp), F32),
            pltpu.VMEM((half, half), BF16),
            pltpu.VMEM((half, half), BF16),
            pltpu.VMEM((nb, n_loc), F32),
            pltpu.VMEM((T, nch, rc, n_loc), F32),
        ] + [dma((nch, q))] * 2 + [dma((nch, R))] * 4 + [dma((nch, q))] * 2 + [dma((q,))] * 2 + [dma((R,))] * 4 + [dma((nch,)), dma, dma((T, nch))],
        compiler_params=pltpu.CompilerParams(
            collective_id=0, has_side_effects=True, vmem_limit_bytes=60 * 2**20),
    )(amplitudes.reshape(T, nch, rc, n_loc), integrals, pair_irrep.reshape(1, R * nb), occ_gap.reshape(1, rows), virt_gap.reshape(1, n_loc))
    return update.reshape(rows, n_loc)


def solution(mesh):
    placed = (P("row", "col"), P("row", "col"), P(), P("row"), P("col"))
    return jax.shard_map(
        functools.partial(body, mesh.shape["row"], mesh.shape["col"]),
        mesh=mesh, in_specs=placed, out_specs=P("row", "col"), check_vma=False,
    )
```

```python
import functools

import jax
import jax.numpy as jnp
from jax import lax
from jax.experimental import pallas as pl
from jax.experimental.pallas import tpu as pltpu
from jax.sharding import PartitionSpec as P

IRREPS = 8
MESH = pl.DeviceIdType.MESH
BF16, F32 = jnp.bfloat16, jnp.float32
NN = (((1,), (0,)), ((), ()))
NT = (((1,), (1,)), ((), ()))


def split(x):
    high = x.astype(BF16)
    return high, (x - high.astype(F32)).astype(BF16)


def dot(a, b, dims=NN):
    return lax.dot_general(a, b, dims, preferred_element_type=F32)


def kernel(sizes, a_ref, v_ref, irr_ref, out_ref, pos, pick, own, own_t, apart, fsend, frecv, lsend, lpart,
           vsrc, vin, vsum, vg, vhigh, vlow, v_in, stage, *sems):
    R, q, G, T, b, bp, nch, rc, n_loc, nb = sizes
    a_s, a_r, f_s, f_r, l_s, l_r, o_s, o_r, x_s, x_r, z_s, z_r, r_s, r_r, own_sem, v_sem, out_sem = sems
    r, c = lax.axis_index("row"), lax.axis_index("col")
    z, s = c // q, c % q
    half = R * b

    def in_group(d):
        return (r, z * q + (s + d) % q)

    def across(d):
        if R & (R - 1):
            return (z + d) % R
        flips = [w for w in (2**k for k in range(R.bit_length())) if (R - d) & w]
        return z + sum(w - 2 * w * ((z // w) % 2) for w in flips)

    def in_line(d):
        return (r, across(d) * q + s)

    def in_plane(d):
        return ((r + d) % R, c)

    def remote(src, dst, send, recv, target):
        return pltpu.make_async_remote_copy(
            src_ref=src, dst_ref=dst, send_sem=send, recv_sem=recv, device_id=target, device_id_type=MESH)

    def a_copy(i, d):
        return remote(a_ref.at[((s + d) % q) // G, i], apart.at[s, i], a_s.at[i, d], a_r.at[i, d], in_group(d))

    def f_copy(i, d):
        return remote(fsend.at[i, across(d)], frecv.at[i, z], f_s.at[i, d], f_r.at[i, d], in_line(d))

    def l_copy(i, d):
        return remote(lsend.at[i, across(d)], lpart.at[s, i, z], l_s.at[i, d], l_r.at[i, d], in_line(d))

    def o_copy(i, d):
        return remote(lpart.at[s, i], lpart.at[s, i], o_s.at[i, d], o_r.at[i, d], in_group(d))

    def x_copy(d):
        return remote(vsrc.at[((s + d) % q) % G], vin.at[s], x_s.at[d], x_r.at[d], in_group(d))

    def z_copy(d):
        return remote(vsum.at[across(d)], vg.at[r, z], z_s.at[d], z_r.at[d], in_line(d))

    def r_copy(d):
        return remote(vg.at[r], vg.at[r], r_s.at[d], r_r.at[d], in_plane(d))

    def own_copy(i):
        return pltpu.make_async_copy(a_ref.at[s // G, i], apart.at[s, i], own_sem.at[i])

    def out_copy(t, i):
        return pltpu.make_async_copy(stage.at[t, i], out_ref.at[t, i], out_sem.at[t, i])

    v_copy = pltpu.make_async_copy(v_ref, v_in, v_sem)

    barrier = pltpu.get_barrier_semaphore()
    for d in range(1, q):
        pl.semaphore_signal(barrier, inc=1, device_id=in_group(d), device_id_type=MESH)
    for d in range(1, R):
        pl.semaphore_signal(barrier, inc=1, device_id=in_line(d), device_id_type=MESH)
        pl.semaphore_signal(barrier, inc=1, device_id=in_plane(d), device_id_type=MESH)
    pl.semaphore_wait(barrier, q - 1 + 2 * (R - 1))

    @pl.loop(0, nch)
    def _(i):
        for d in range(1, q):
            a_copy(i, d).start()
        own_copy(i).start()

    v_copy.start()

    before = (lax.broadcasted_iota(jnp.int32, (nb, nb), 0) < lax.broadcasted_iota(jnp.int32, (nb, nb), 1)).astype(F32).astype(BF16)

    def slots(block):
        labels = irr_ref[:, pl.ds(pl.multiple_of(block * nb, 128), nb)]
        mine = (lax.broadcasted_iota(jnp.int32, (IRREPS, nb), 0) == labels).astype(F32)
        rank = jnp.sum(mine * dot(mine.astype(BF16), before), axis=0, keepdims=True).astype(jnp.int32)
        return (labels % G) * half + (labels // G) * b + rank

    pos_n = slots(z)
    pos[0:1, :] = pos_n
    pick[...] = (lax.broadcasted_iota(jnp.int32, (half, nb), 0) + (s % G) * half == pos_n).astype(F32).astype(BF16)

    def forward(i):
        own_copy(i).wait()
        for d in range(1, q):
            a_copy(i, d).wait_recv()
        total = jnp.zeros((half, rc), F32)
        for j in range(q):
            high, low = split(apart[j, i])
            chosen = pick[:, j * n_loc:(j + 1) * n_loc]
            total += dot(chosen, high, NT) + dot(chosen, low, NT)
        fsend[i] = total.reshape(R, b, rc)
        for d in range(1, R):
            f_copy(i, d).start()
        frecv[i, z] = fsend[i, z]

    forward(0)

    pos_own = pos[0:1, pl.ds(pl.multiple_of(s * n_loc, 128), n_loc)]
    own_f = (lax.broadcasted_iota(jnp.int32, (IRREPS * b, n_loc), 0) == pos_own).astype(F32)
    own[...] = own_f.astype(BF16)
    pos_k = slots(r)
    v_copy.wait()
    v_high, v_low = split(v_in[...])
    vsrc[...] = jnp.zeros_like(vsrc)
    for p in range(G):
        rows = (lax.broadcasted_iota(jnp.int32, (half, nb), 0) + p * half == pos_k).astype(F32).astype(BF16)
        sorted_v = dot(rows, v_high) + dot(rows, v_low)
        for j in range(R):
            high, low = split(sorted_v[j * b:(j + 1) * b, :])
            chosen = own[p * half + j * b:p * half + (j + 1) * b, :]
            vsrc[p, j, :, 0:b] = dot(chosen, high, NT) + dot(chosen, low, NT)
    for d in range(1, q):
        x_copy(d).start()
    vin[s] = vsrc[s % G]

    @pl.loop(1, 2)
    def _(i):
        forward(i)

    for d in range(1, q):
        x_copy(d).wait_recv()
    block = vin[0]
    for j in range(1, q):
        block += vin[j]
    vsum[...] = block
    for d in range(1, R):
        z_copy(d).start()
    vg[r, z] = vsum[z]

    @pl.loop(2, nch)
    def _(i):
        forward(i)

    own_t[...] = own_f.T.astype(BF16)
    for d in range(1, R):
        z_copy(d).wait_recv()
    for d in range(1, R):
        r_copy(d).start()
    for d in range(1, R):
        r_copy(d).wait_recv()
    whole = jnp.concatenate([vg[j].reshape(half, bp)[:, :b] for j in range(R)], axis=1)
    high, low = split(whole)
    vhigh[...] = high
    vlow[...] = low

    @pl.loop(0, nch)
    def _(i):
        for d in range(1, R):
            f_copy(i, d).wait_recv()
        high, low = split(frecv[i].reshape(half, rc))
        total = dot(vhigh[...], high) + (dot(vhigh[...], low) + dot(vlow[...], high))
        lsend[i] = total.reshape(R, b, rc)
        for d in range(1, R):
            l_copy(i, d).start()
        lpart[s, i, z] = lsend[i, z]

    def share(i):
        for d in range(1, R):
            l_copy(i, d).wait_recv()
        for d in range(1, q):
            o_copy(i, d).start()

    def finish(i):
        for d in range(1, q):
            o_copy(i, d).wait_recv()
        for t in range(T):
            total = jnp.zeros((n_loc, rc), F32)
            for p in range(G):
                high, low = split(lpart[t * G + p, i].reshape(half, rc))
                chosen = own_t[:, p * half:(p + 1) * half]
                total += dot(chosen, high) + dot(chosen, low)
            stage[t, i] = total.T
            out_copy(t, i).start()

    share(0)

    @pl.loop(1, nch)
    def _(i):
        share(i)
        finish(i - 1)

    finish(nch - 1)

    @pl.loop(0, nch)
    def _(i):
        for d in range(1, q):
            a_copy(i, d).wait_send()
            o_copy(i, d).wait_send()
        for t in range(T):
            out_copy(t, i).wait()
        for d in range(1, R):
            f_copy(i, d).wait_send()
            l_copy(i, d).wait_send()

    for d in range(1, q):
        x_copy(d).wait_send()
    for d in range(1, R):
        z_copy(d).wait_send()
        r_copy(d).wait_send()


def body(R, C, amplitudes, integrals, pair_irrep, occ_gap, virt_gap):
    rows, n_loc = amplitudes.shape
    nb = integrals.shape[0]
    q, G = C // R, IRREPS // R
    T = q // G
    b = nb // IRREPS
    bp = -(-b // 128) * 128
    rc = 128
    nch = rows // T // rc
    half = R * b
    sizes = (R, q, G, T, b, bp, nch, rc, n_loc, nb)
    dma = pltpu.SemaphoreType.DMA
    ladder = pl.pallas_call(
        functools.partial(kernel, sizes),
        out_shape=jax.ShapeDtypeStruct((T, nch, rc, n_loc), F32),
        in_specs=[pl.BlockSpec(memory_space=pl.ANY)] * 2 + [pl.BlockSpec(memory_space=pltpu.VMEM)],
        out_specs=pl.BlockSpec(memory_space=pl.ANY),
        scratch_shapes=[
            pltpu.VMEM((8, nb), jnp.int32),
            pltpu.VMEM((half, nb), BF16),
            pltpu.VMEM((IRREPS * b, n_loc), BF16),
            pltpu.VMEM((n_loc, IRREPS * b), BF16),
            pltpu.VMEM((q, nch, rc, n_loc), F32),
            pltpu.VMEM((nch, R, b, rc), F32),
            pltpu.VMEM((nch, R, b, rc), F32),
            pltpu.VMEM((nch, R, b, rc), F32),
            pltpu.VMEM((q, nch, R, b, rc), F32),
            pltpu.VMEM((G, R, b, bp), F32),
            pltpu.VMEM((q, R, b, bp), F32),
            pltpu.VMEM((R, b, bp), F32),
            pltpu.VMEM((R, R, b, bp), F32),
            pltpu.VMEM((half, half), BF16),
            pltpu.VMEM((half, half), BF16),
            pltpu.VMEM((nb, n_loc), F32),
            pltpu.VMEM((T, nch, rc, n_loc), F32),
        ] + [dma((nch, q))] * 2 + [dma((nch, R))] * 4 + [dma((nch, q))] * 2 + [dma((q,))] * 2 + [dma((R,))] * 4 + [dma((nch,)), dma, dma((T, nch))],
        compiler_params=pltpu.CompilerParams(
            collective_id=0, has_side_effects=True, vmem_limit_bytes=60 * 2**20),
    )(amplitudes.reshape(T, nch, rc, n_loc), integrals, pair_irrep.reshape(1, R * nb))
    return ladder.reshape(rows, n_loc) / (occ_gap[:, None] + virt_gap[None, :])


def solution(mesh):
    placed = (P("row", "col"), P("row", "col"), P(), P("row"), P("col"))
    return jax.shard_map(
        functools.partial(body, mesh.shape["row"], mesh.shape["col"]),
        mesh=mesh, in_specs=placed, out_specs=P("row", "col"), check_vma=False,
    )
```

```python
import functools

import jax
import jax.numpy as jnp
from jax import lax
from jax.experimental import pallas as pl
from jax.experimental.pallas import tpu as pltpu
from jax.sharding import PartitionSpec as P

IRREPS = 8
MESH = pl.DeviceIdType.MESH
BF16, F32 = jnp.bfloat16, jnp.float32
NN = (((1,), (0,)), ((), ()))
NT = (((1,), (1,)), ((), ()))


def split(x):
    high = x.astype(BF16)
    return high, (x - high.astype(F32)).astype(BF16)


def dot(a, b, dims=NN):
    return lax.dot_general(a, b, dims, preferred_element_type=F32)


def kernel(sizes, a_ref, v_ref, irr_ref, out_ref, pos, pick, own, own_t, apart, fsend, frecv, lsend, lpart,
           vsrc, vin, vsum, vg, vhigh, vlow, v_in, stage, *sems):
    R, q, G, T, b, bp, nch, rc, n_loc, nb = sizes
    a_s, a_r, f_s, f_r, l_s, l_r, o_s, o_r, x_s, x_r, z_s, z_r, r_s, r_r, own_sem, v_sem, out_sem = sems
    r, c = lax.axis_index("row"), lax.axis_index("col")
    z, s = c // q, c % q
    half = R * b

    def in_group(d):
        return (r, z * q + (s + d) % q)

    def across(d):
        if R & (R - 1):
            return (z + d) % R
        flips = [w for w in (2**k for k in range(R.bit_length())) if (R - d) & w]
        return z + sum(w - 2 * w * ((z // w) % 2) for w in flips)

    def in_line(d):
        return (r, across(d) * q + s)

    def in_plane(d):
        return ((r + d) % R, c)

    def remote(src, dst, send, recv, target):
        return pltpu.make_async_remote_copy(
            src_ref=src, dst_ref=dst, send_sem=send, recv_sem=recv, device_id=target, device_id_type=MESH)

    def a_copy(i, d):
        return remote(a_ref.at[((s + d) % q) // G, i], apart.at[s, i], a_s.at[i, d], a_r.at[i, d], in_group(d))

    def f_copy(i, d):
        return remote(fsend.at[i, across(d)], frecv.at[i, z], f_s.at[i, d], f_r.at[i, d], in_line(d))

    def l_copy(i, d):
        return remote(lsend.at[i, across(d)], lpart.at[s, i, z], l_s.at[i, d], l_r.at[i, d], in_line(d))

    def o_copy(i, d):
        return remote(lpart.at[s, i], lpart.at[s, i], o_s.at[i, d], o_r.at[i, d], in_group(d))

    def x_copy(d):
        return remote(vsrc.at[((s + d) % q) % G], vin.at[s], x_s.at[d], x_r.at[d], in_group(d))

    def z_copy(d):
        return remote(vsum.at[across(d)], vg.at[r, z], z_s.at[d], z_r.at[d], in_line(d))

    def r_copy(d):
        return remote(vg.at[r], vg.at[r], r_s.at[d], r_r.at[d], in_plane(d))

    def own_copy(i):
        return pltpu.make_async_copy(a_ref.at[s // G, i], apart.at[s, i], own_sem.at[i])

    def out_copy(t, i):
        return pltpu.make_async_copy(stage.at[t, i], out_ref.at[t, i], out_sem.at[t, i])

    v_copy = pltpu.make_async_copy(v_ref, v_in, v_sem)

    barrier = pltpu.get_barrier_semaphore()
    for d in range(1, q):
        pl.semaphore_signal(barrier, inc=1, device_id=in_group(d), device_id_type=MESH)
    for d in range(1, R):
        pl.semaphore_signal(barrier, inc=1, device_id=in_line(d), device_id_type=MESH)
        pl.semaphore_signal(barrier, inc=1, device_id=in_plane(d), device_id_type=MESH)
    pl.semaphore_wait(barrier, q - 1 + 2 * (R - 1))

    @pl.loop(0, nch)
    def _(i):
        for d in range(1, q):
            a_copy(i, d).start()
        own_copy(i).start()

    v_copy.start()

    before = (lax.broadcasted_iota(jnp.int32, (nb, nb), 0) < lax.broadcasted_iota(jnp.int32, (nb, nb), 1)).astype(F32).astype(BF16)

    def slots(block):
        labels = irr_ref[:, pl.ds(pl.multiple_of(block * nb, 128), nb)]
        mine = (lax.broadcasted_iota(jnp.int32, (IRREPS, nb), 0) == labels).astype(F32)
        rank = jnp.sum(mine * dot(mine.astype(BF16), before), axis=0, keepdims=True).astype(jnp.int32)
        return (labels % G) * half + (labels // G) * b + rank

    pos_n = slots(z)
    pos[0:1, :] = pos_n
    pick[...] = (lax.broadcasted_iota(jnp.int32, (half, nb), 0) + (s % G) * half == pos_n).astype(F32).astype(BF16)

    def forward(i):
        own_copy(i).wait()
        for d in range(1, q):
            a_copy(i, d).wait_recv()
        total = jnp.zeros((half, rc), F32)
        for j in range(q):
            high, low = split(apart[j, i])
            chosen = pick[:, j * n_loc:(j + 1) * n_loc]
            total += dot(chosen, high, NT) + dot(chosen, low, NT)
        fsend[i] = total.reshape(R, b, rc)
        for d in range(1, R):
            f_copy(i, d).start()
        frecv[i, z] = fsend[i, z]

    forward(0)

    pos_own = pos[0:1, pl.ds(pl.multiple_of(s * n_loc, 128), n_loc)]
    own_f = (lax.broadcasted_iota(jnp.int32, (IRREPS * b, n_loc), 0) == pos_own).astype(F32)
    own[...] = own_f.astype(BF16)
    pos_k = slots(r)
    v_copy.wait()
    v_high, v_low = split(v_in[...])
    vsrc[...] = jnp.zeros_like(vsrc)
    for p in range(G):
        rows = (lax.broadcasted_iota(jnp.int32, (half, nb), 0) + p * half == pos_k).astype(F32).astype(BF16)
        sorted_v = dot(rows, v_high) + dot(rows, v_low)
        for j in range(R):
            high, low = split(sorted_v[j * b:(j + 1) * b, :])
            chosen = own[p * half + j * b:p * half + (j + 1) * b, :]
            vsrc[p, j, :, 0:b] = dot(chosen, high, NT) + dot(chosen, low, NT)
    for d in range(1, q):
        x_copy(d).start()
    vin[s] = vsrc[s % G]

    @pl.loop(1, 2)
    def _(i):
        forward(i)

    for d in range(1, q):
        x_copy(d).wait_recv()
    block = vin[0]
    for j in range(1, q):
        block += vin[j]
    vsum[...] = block
    for d in range(1, R):
        z_copy(d).start()
    vg[r, z] = vsum[z]

    @pl.loop(2, nch)
    def _(i):
        forward(i)

    own_t[...] = own_f.T.astype(BF16)
    for d in range(1, R):
        z_copy(d).wait_recv()
    for d in range(1, R):
        r_copy(d).start()
    for d in range(1, R):
        r_copy(d).wait_recv()
    whole = jnp.concatenate([vg[j].reshape(half, bp)[:, :b] for j in range(R)], axis=1)
    high, low = split(whole)
    vhigh[...] = high
    vlow[...] = low

    @pl.loop(0, nch)
    def _(i):
        for d in range(1, R):
            f_copy(i, d).wait_recv()
        high, low = split(frecv[i].reshape(half, rc))
        total = dot(vhigh[...], high) + (dot(vhigh[...], low) + dot(vlow[...], high))
        lsend[i] = total.reshape(R, b, rc)
        for d in range(R - 1, 0, -1):
            l_copy(i, d).start()
        lpart[s, i, z] = lsend[i, z]

    def share(i):
        for d in range(1, R):
            l_copy(i, d).wait_recv()
        for d in range(1, q):
            o_copy(i, d).start()

    def finish(i):
        for d in range(1, q):
            o_copy(i, d).wait_recv()
        for t in range(T):
            total = jnp.zeros((n_loc, rc), F32)
            for p in range(G):
                high, low = split(lpart[t * G + p, i].reshape(half, rc))
                chosen = own_t[:, p * half:(p + 1) * half]
                total += dot(chosen, high) + dot(chosen, low)
            stage[t, i] = total.T
            out_copy(t, i).start()

    share(0)

    @pl.loop(1, nch)
    def _(i):
        share(i)
        finish(i - 1)

    finish(nch - 1)

    @pl.loop(0, nch)
    def _(i):
        for d in range(1, q):
            a_copy(i, d).wait_send()
            o_copy(i, d).wait_send()
        for t in range(T):
            out_copy(t, i).wait()
        for d in range(1, R):
            f_copy(i, d).wait_send()
            l_copy(i, d).wait_send()

    for d in range(1, q):
        x_copy(d).wait_send()
    for d in range(1, R):
        z_copy(d).wait_send()
        r_copy(d).wait_send()


def body(R, C, amplitudes, integrals, pair_irrep, occ_gap, virt_gap):
    rows, n_loc = amplitudes.shape
    nb = integrals.shape[0]
    q, G = C // R, IRREPS // R
    T = q // G
    b = nb // IRREPS
    bp = -(-b // 128) * 128
    rc = 128
    nch = rows // T // rc
    half = R * b
    sizes = (R, q, G, T, b, bp, nch, rc, n_loc, nb)
    dma = pltpu.SemaphoreType.DMA
    ladder = pl.pallas_call(
        functools.partial(kernel, sizes),
        out_shape=jax.ShapeDtypeStruct((T, nch, rc, n_loc), F32),
        in_specs=[pl.BlockSpec(memory_space=pl.ANY)] * 2 + [pl.BlockSpec(memory_space=pltpu.VMEM)],
        out_specs=pl.BlockSpec(memory_space=pl.ANY),
        scratch_shapes=[
            pltpu.VMEM((8, nb), jnp.int32),
            pltpu.VMEM((half, nb), BF16),
            pltpu.VMEM((IRREPS * b, n_loc), BF16),
            pltpu.VMEM((n_loc, IRREPS * b), BF16),
            pltpu.VMEM((q, nch, rc, n_loc), F32),
            pltpu.VMEM((nch, R, b, rc), F32),
            pltpu.VMEM((nch, R, b, rc), F32),
            pltpu.VMEM((nch, R, b, rc), F32),
            pltpu.VMEM((q, nch, R, b, rc), F32),
            pltpu.VMEM((G, R, b, bp), F32),
            pltpu.VMEM((q, R, b, bp), F32),
            pltpu.VMEM((R, b, bp), F32),
            pltpu.VMEM((R, R, b, bp), F32),
            pltpu.VMEM((half, half), BF16),
            pltpu.VMEM((half, half), BF16),
            pltpu.VMEM((nb, n_loc), F32),
            pltpu.VMEM((T, nch, rc, n_loc), F32),
        ] + [dma((nch, q))] * 2 + [dma((nch, R))] * 4 + [dma((nch, q))] * 2 + [dma((q,))] * 2 + [dma((R,))] * 4 + [dma((nch,)), dma, dma((T, nch))],
        compiler_params=pltpu.CompilerParams(
            collective_id=0, has_side_effects=True, vmem_limit_bytes=60 * 2**20),
    )(amplitudes.reshape(T, nch, rc, n_loc), integrals, pair_irrep.reshape(1, R * nb))
    return ladder.reshape(rows, n_loc) / (occ_gap[:, None] + virt_gap[None, :])


def solution(mesh):
    placed = (P("row", "col"), P("row", "col"), P(), P("row"), P("col"))
    return jax.shard_map(
        functools.partial(body, mesh.shape["row"], mesh.shape["col"]),
        mesh=mesh, in_specs=placed, out_specs=P("row", "col"), check_vma=False,
    )
```
